32 devices in a mesh: dp: 4 (over y, x), row: 2 (over core), col: 4 (over z).
Axes of the slice: x: 2, y: 2, z: 4, core: 2. Of those that a mesh axis runs over, the one named last changes fastest.
Arguments:
- hidden: bfloat16 [4096, 14336], P('dp', 'row'), may hold values from -6 to 6
- upstream: bfloat16 [4096, 4096], P('dp', 'col'), may hold values from -0.09375 to 0.09375
- first_codes: int32 [14336, 4096], P(('row', 'dp'), 'col'), may hold values from 0 to 15
- first_scale: float32 [14336, 32], P(('row', 'dp'), 'col'), may hold values from 0.1 to 1
- second_codes: int32 [14336, 4096], P(('row', 'dp'), 'col'), may hold values from 0 to 15
- second_rows: float32 [14336], P(('row', 'dp')), may hold values from 0.004 to 0.04
- second_columns: float32 [4096], P('col'), may hold values from 0.004 to 0.04
Outputs:
- update_step: float32 [14336, 4096], P(('row', 'dp'), 'col')
- first_normed: bfloat16 [14336, 4096], P(('row', 'dp'), 'col')
- first_peak: float32 [14336, 32], P(('row', 'dp'), 'col')
- second_normed: bfloat16 [14336, 4096], P(('row', 'dp'), 'col')
- row_peak: float32 [14336], P(('row', 'dp'))
- column_peak: float32 [4096], P('col')
The draws below stay inside these ranges and needn't reach their ends.
All inputs are finite; a program needn't handle non-finite values. Where the reference program divides by a largest or mean magnitude, that divisor is 1e-20 or more.
Results may differ from the reference program's by a relative error of at most 0.015.
Values may be sent and summed in bfloat16 or wider, within the bound.
A program may use at most 128 MiB of HBM per device.

```python
import math
import jax
import jax.numpy as jnp
from jax import lax

FFW = 14336
DW = 4096
BLOCK = 128
STEP = 10
TOK_DEV = 1024
TOKENS = 4096
N_DP = 4


def place_ends(entries, key, smallest, high):
    place = [jax.random.randint(jax.random.fold_in(key, axis), (), 0, length) for axis, length in enumerate(entries.shape)]
    longest = entries.shape.index(max(entries.shape))
    next_to = place[:longest] + [(place[longest] + 1) % entries.shape[longest]] + place[longest + 1:]
    return entries.at[tuple(place)].set(smallest).at[tuple(next_to)].set(high)


def level_of(rng, extent, split, smallest, largest):
    def one(position, blocks):
        heights = jax.random.uniform(jax.random.fold_in(jax.random.fold_in(rng, 6), position), (blocks,), jnp.float32, smallest / len(split), largest / len(split))
        return jnp.repeat(jnp.exp(heights), extent[position] // blocks).reshape((-1,) + (1,) * (len(extent) - position - 1))

    level = one(*split[0])
    for cut in split[1:]:
        level = level * one(*cut)
    return level


def centred(stream_key, shape, spread, bound, pieces=(), kind=jnp.bfloat16):
    level = level_of(stream_key, shape, pieces, -0.22, 0.18) if pieces else 1.0
    array = jax.random.normal(stream_key, shape, jnp.float32) * spread * level
    return jnp.minimum(jnp.maximum(array, -bound), bound).astype(kind)


def setup_inputs(seed: int = 0) -> dict:
    splits = jax.random.split(jax.random.key(seed), 8)
    hidden = centred(splits[0], (TOKENS, FFW), 1.0, 6.0, ((0, 4), (1, 2)))
    upstream = centred(splits[1], (TOKENS, DW), TOKENS ** -0.5, 0.09375, ((0, 4), (1, 4)))
    first_codes = place_ends(jax.random.randint(splits[2], (FFW, DW), 0, 16), jax.random.fold_in(splits[2], 1), 0, 15).astype(jnp.int32)
    first_scale = jnp.clip(jnp.exp(math.log(1.0) - 2.3025851 * jax.random.uniform(splits[3], (FFW, DW // BLOCK), jnp.float32) ** level_of(splits[3], (FFW, DW // BLOCK), ((0, 8), (1, 4)), -0.2, 0.2)), 0.1, 1.0)
    second_codes = place_ends(jax.random.randint(splits[4], (FFW, DW), 0, 16), jax.random.fold_in(splits[4], 1), 0, 15).astype(jnp.int32)
    second_rows = jnp.clip(jnp.exp(math.log(0.04) - 2.30258502 * jax.random.uniform(splits[5], (FFW,), jnp.float32) ** level_of(splits[5], (FFW,), ((0, 8),), -0.2, 0.2)), 0.004, 0.04)
    second_columns = jnp.clip(jnp.exp(math.log(0.04) - 2.30258502 * jax.random.uniform(splits[6], (DW,), jnp.float32) ** level_of(splits[6], (DW,), ((0, 4),), -0.2, 0.2)), 0.004, 0.04)
    return {"hidden": hidden, "upstream": upstream, "first_codes": first_codes, "first_scale": first_scale, "second_codes": second_codes, "second_rows": second_rows, "second_columns": second_columns}


def first_table(codes):
    level = codes.astype(jnp.float32)
    upper = level >= 8.0
    expo = jnp.where(upper, level - 8.0, 7.0 - level)
    magnitude = jnp.where(expo > 0.0, jnp.exp2(expo - 7.0), 0.0 * expo)
    return jnp.where(upper, magnitude, -magnitude)

def reference(hidden, upstream, first_codes, first_scale, second_codes, second_rows, second_columns):
    grouped_hidden = hidden.reshape(N_DP, TOK_DEV, FFW)
    grouped_upstream = upstream.reshape(N_DP, TOK_DEV, DW)

    def add_group(total, pair):
        left, right = pair
        partial_value = jnp.dot(left.T, right, preferred_element_type=jnp.float32).astype(jnp.bfloat16)
        return (total + partial_value.astype(jnp.float32), None)
    gradient, _ = lax.scan(add_group, jnp.zeros((FFW, DW), jnp.float32), (grouped_hidden, grouped_upstream))
    block_count = first_scale.shape[1]
    shaped = gradient.reshape(FFW, block_count, -1)
    first_old = first_scale[:, :, None] * first_table(first_codes).reshape(FFW, block_count, -1)
    level_two = (second_codes.astype(jnp.float32) + 1.0) / 16.0
    second_old = jnp.minimum(second_rows[:, None], second_columns[None, :]) * level_two
    second_old = second_old.reshape(FFW, block_count, -1)
    first_new = 0.9 * first_old + 0.1 * shaped
    second_new = 0.999 * second_old + 0.001 * shaped * shaped
    corr_one = 1.0 - 0.9 ** STEP
    corr_two = 1.0 - 0.999 ** STEP
    update_step = first_new / corr_one / (jnp.sqrt(second_new / corr_two) + 1e-08)
    first_peak = lax.optimization_barrier(jnp.max(jnp.abs(first_new), axis=2))
    first_normed = (first_new / (first_peak[:, :, None] + 1e-06)).astype(jnp.bfloat16)
    second_flat = second_new.reshape(FFW, DW)
    row_peak = lax.optimization_barrier(jnp.max(second_flat, axis=1))
    column_peak = lax.optimization_barrier(jnp.max(second_flat, axis=0))
    second_normed = (second_flat / (jnp.minimum(row_peak[:, None], column_peak[None, :]) + 1e-06)).astype(jnp.bfloat16)
    return (update_step.reshape(FFW, DW), first_normed.reshape(FFW, DW), first_peak, second_normed, row_peak, column_peak)
```

```python
import functools

import jax
import jax.numpy as jnp
from jax import lax
from jax.experimental import pallas as pl
from jax.experimental.pallas import tpu as pltpu
from jax.sharding import PartitionSpec as P

STEP = 10
CORR_ONE = 1.0 - 0.9**STEP
CORR_TWO = 1.0 - 0.999**STEP
LANES = 128
PARTS = 4
MESH = pl.DeviceIdType.MESH


def contract_tokens(left, right):
    return lax.dot_general(
        left, right, (((0,), (0,)), ((), ())), preferred_element_type=jnp.float32
    )


def update_kernel(
    start, blocks, terms, first, codes_one, scale_ref, codes_two, rows_ref, columns_ref, *refs
):
    term_refs, refs = refs[:terms], refs[terms:]
    if not first:
        row_in, peak_in = refs[3:5]
        refs = refs[5:]
    update_ref, normed_ref, second_ref, row_ref, peak_ref, column_ref = refs
    rows = codes_one.shape[0]
    second_rows = rows_ref[...]
    row_part = None if first else row_in[...]
    if not first:
        peak_ref[...] = peak_in[...]
    for block in range(blocks):
        at = pl.ds(block * LANES, LANES)
        gradient = term_refs[0][:, at].astype(jnp.float32)
        for term in term_refs[1:]:
            gradient += term[:, at].astype(jnp.float32)
        level = codes_one[:, at].astype(jnp.float32)
        upper = level >= 8.0
        expo = jnp.where(upper, level - 8.0, 7.0 - level)
        magnitude = jnp.where(expo > 0.0, jnp.exp2(expo - 7.0), 0.0)
        table = jnp.where(upper, magnitude, -magnitude)
        first_new = (0.9 * scale_ref[:, start + block : start + block + 1]) * table + 0.1 * gradient
        level_two = codes_two[:, at].astype(jnp.float32) * (0.999 / 16.0) + (0.999 / 16.0)
        second_new = (
            jnp.minimum(second_rows, columns_ref[:, at]) * level_two + 0.001 * gradient * gradient
        )
        update_ref[:, at] = (first_new * (1.0 / CORR_ONE)) / (
            jnp.sqrt(second_new * (1.0 / CORR_TWO)) + 1e-08
        )
        peak = jnp.max(jnp.abs(first_new), axis=1, keepdims=True)
        peak_ref[:, start + block : start + block + 1] = peak
        normed_ref[:, at] = (first_new * (1.0 / (peak + 1e-06))).astype(jnp.bfloat16)
        second_ref[:, at] = second_new
        row_part = second_new if row_part is None else jnp.maximum(row_part, second_new)
        column_part = jnp.max(second_new.reshape(rows // 8, 8, LANES), axis=0)

        @pl.when(pl.program_id(0) == 0)
        def _():
            column_ref[:, at] = column_part

        @pl.when(pl.program_id(0) > 0)
        def _():
            column_ref[:, at] = jnp.maximum(column_ref[:, at], column_part)

    row_ref[...] = row_part


def update_part(part, parts, terms, codes_one, scale, codes_two, rows, columns, carried):
    total, width = codes_one.shape
    wide = width // parts
    blocks = wide // LANES
    tall = next(t for t in (256, 224, 192, 128, 112, 64, 32, 16) if total % t == 0)
    here = pl.BlockSpec((tall, wide), lambda i: (i, part))
    specs = [
        here,
        pl.BlockSpec((tall, scale.shape[1]), lambda i: (i, 0)),
        here,
        pl.BlockSpec((tall, 1), lambda i: (i, 0)),
        pl.BlockSpec((1, wide), lambda i: (0, part)),
    ]
    specs += [pl.BlockSpec((tall, wide), lambda i: (i, 0))] * len(terms)
    by_rows = pl.BlockSpec((tall, LANES), lambda i: (i, 0))
    by_blocks = pl.BlockSpec((tall, scale.shape[1]), lambda i: (i, 0))
    operands = [codes_one, scale, codes_two, rows, columns] + terms
    aliases = {}
    if carried is not None:
        aliases = {len(operands) + k: k for k in range(5)}
        operands += list(carried)
        specs += [pl.BlockSpec(memory_space=pl.ANY)] * 3 + [by_rows, by_blocks]
    size = total * wide
    return pl.pallas_call(
        functools.partial(update_kernel, part * blocks, blocks, len(terms), carried is None),
        grid=(total // tall,),
        in_specs=specs,
        out_specs=[
            here,
            here,
            here,
            by_rows,
            by_blocks,
            pl.BlockSpec((8, wide), lambda i: (0, 0)),
        ],
        out_shape=[
            jax.ShapeDtypeStruct((total, width), jnp.float32),
            jax.ShapeDtypeStruct((total, width), jnp.bfloat16),
            jax.ShapeDtypeStruct((total, width), jnp.float32),
            jax.ShapeDtypeStruct((total, LANES), jnp.float32),
            jax.ShapeDtypeStruct(scale.shape, jnp.float32),
            jax.ShapeDtypeStruct((8, wide), jnp.float32),
        ],
        input_output_aliases=aliases,
        compiler_params=pltpu.CompilerParams(vmem_limit_bytes=56 * 2**20),
        cost_estimate=pl.CostEstimate(
            flops=40 * size, bytes_accessed=20 * size, transcendentals=3 * size
        ),
    )(*operands)


def peaks_kernel(
    sizes, row_ref, column_ref, row_out, column_out, row_held, column_held, rs, rr, cs, cr
):
    n_dp, n_row, n_col = sizes
    dp, row, col = lax.axis_index("dp"), lax.axis_index("row"), lax.axis_index("col")
    plane = n_dp * n_row
    me = dp * n_row + row
    along = [{"dp": dp, "row": row, "col": lax.rem(col + d, n_col)} for d in range(1, n_col)]
    across = []
    for d in range(1, plane):
        peer = lax.rem(me + d, plane)
        across.append({"dp": peer // n_row, "row": lax.rem(peer, n_row), "col": col})
    barrier = pltpu.get_barrier_semaphore()
    for peer in along + across:
        pl.semaphore_signal(barrier, inc=1, device_id=peer, device_id_type=MESH)
    pl.semaphore_wait(barrier, len(along) + len(across))
    copies = []
    for source, held, send, recv, peers in (
        (column_ref, column_held, cs, cr, across),
        (row_ref, row_held, rs, rr, along),
    ):
        for slot, peer in enumerate(peers):
            copy = pltpu.make_async_remote_copy(
                src_ref=source,
                dst_ref=held.at[slot],
                send_sem=send.at[slot],
                recv_sem=recv.at[slot],
                device_id=peer,
                device_id_type=MESH,
            )
            copy.start()
            copies.append(copy)
    for copy in copies:
        copy.wait()
    row_out[...] = jnp.maximum(row_ref[...], jnp.max(row_held[...], axis=0))
    column_out[...] = jnp.maximum(column_ref[...], jnp.max(column_held[...], axis=0))


def exchange_peaks(sizes, row_part, column_part):
    def folded(values):
        short = -values.shape[0] % (8 * LANES)
        return jnp.pad(values, (0, short)).reshape(-1, LANES)

    row_fold, column_fold = folded(row_part), folded(column_part)
    n_dp, n_row, n_col = sizes
    others, beside = n_dp * n_row - 1, n_col - 1
    vmem = pl.BlockSpec(memory_space=pltpu.VMEM)
    row_all, column_all = pl.pallas_call(
        functools.partial(peaks_kernel, sizes),
        out_shape=[
            jax.ShapeDtypeStruct(row_fold.shape, jnp.float32),
            jax.ShapeDtypeStruct(column_fold.shape, jnp.float32),
        ],
        in_specs=[vmem, vmem],
        out_specs=[vmem, vmem],
        scratch_shapes=[
            pltpu.VMEM((beside,) + row_fold.shape, jnp.float32),
            pltpu.VMEM((others,) + column_fold.shape, jnp.float32),
            pltpu.SemaphoreType.DMA((beside,)),
            pltpu.SemaphoreType.DMA((beside,)),
            pltpu.SemaphoreType.DMA((others,)),
            pltpu.SemaphoreType.DMA((others,)),
        ],
        compiler_params=pltpu.CompilerParams(collective_id=0, has_side_effects=True),
    )(row_fold, column_fold)
    return (
        row_all.reshape(-1)[: row_part.shape[0]],
        column_all.reshape(-1)[: column_part.shape[0]],
    )


def scatter_terms(n_dp, partial, side):
    bits = n_dp.bit_length() - 1
    if 1 << bits != n_dp:
        return [lax.psum_scatter(partial, "dp", scatter_dimension=0, tiled=True)]
    me = lax.axis_index("dp")
    shape = (2,) * bits + (partial.shape[0] // n_dp, partial.shape[1])
    terms = [partial.reshape(shape)]
    for step in range(bits):
        axis = 0 if side else bits - 1 - step
        bit = bits - 1 - step if side else step
        mine = lax.rem(me // (1 << bit), 2)
        sent = [lax.dynamic_index_in_dim(t, 1 - mine, axis, keepdims=False) for t in terms]
        terms = [lax.dynamic_index_in_dim(t, mine, axis, keepdims=False) for t in terms]
        total = sent[0].astype(jnp.float32)
        for term in sent[1:]:
            total += term.astype(jnp.float32)
        terms.append(
            lax.ppermute(
                total.astype(jnp.bfloat16), "dp", [(i, i ^ (1 << bit)) for i in range(n_dp)]
            )
        )
    return terms


def per_device(
    sizes, hidden, upstream, first_codes, first_scale, second_codes, second_rows, second_columns
):
    columns = first_codes.shape[1]
    wide = columns // PARTS
    both = columns // (PARTS // 2)
    gathered = []
    for pair in range(PARTS // 2):
        partial = contract_tokens(hidden, upstream[:, pair * both : (pair + 1) * both])
        partial = partial.astype(jnp.bfloat16)
        for side in range(2):
            gathered.append(
                scatter_terms(sizes[0], partial[:, side * wide : (side + 1) * wide], side)
            )
    carried, column_parts = None, []
    for part in range(PARTS):
        *carried, column_part = update_part(
            part,
            PARTS,
            gathered[part],
            first_codes,
            first_scale,
            second_codes,
            second_rows[:, None],
            second_columns[None, :],
            carried,
        )
        column_parts.append(column_part)
    update_step, first_normed, second_new, row_part, first_peak = carried
    row_peak, column_peak = exchange_peaks(
        sizes,
        jnp.max(row_part, axis=1),
        jnp.max(jnp.concatenate(column_parts, axis=1), axis=0),
    )
    second_normed = (
        second_new / (jnp.minimum(row_peak[:, None], column_peak[None, :]) + 1e-06)
    ).astype(jnp.bfloat16)
    return update_step, first_normed, first_peak, second_normed, row_peak, column_peak


def solution(mesh):
    placed = (
        P("dp", "row"),
        P("dp", "col"),
        P(("row", "dp"), "col"),
        P(("row", "dp"), "col"),
        P(("row", "dp"), "col"),
        P(("row", "dp")),
        P("col"),
    )
    sizes = (mesh.shape["dp"], mesh.shape["row"], mesh.shape["col"])
    return jax.shard_map(
        functools.partial(per_device, sizes),
        mesh=mesh,
        in_specs=placed,
        out_specs=(
            P(("row", "dp"), "col"),
            P(("row", "dp"), "col"),
            P(("row", "dp"), "col"),
            P(("row", "dp"), "col"),
            P(("row", "dp")),
            P("col"),
        ),
        check_vma=False,
    )
```
